128 devices in a mesh: rows: 16 (over y, x), cols: 8 (over z, core).
Axes of the slice: x: 4, y: 4, z: 4, core: 2. Of those that a mesh axis runs over, the one named last changes fastest.
Arguments:
- memory: float32 [128, 524288], P('cols', 'rows'), may hold values from -3 to 3
- last_tick: int32 [524288], P('rows'), may hold values from 0 to 999
- slot_node: int32 [256, 256], P('rows'), may hold values from 0 to 524287, as said below
- slot_pair: int32 [256, 256], P('rows'), may hold values from 0 to 4095, as said below
- slot_tick: int32 [256, 256], P('rows'), may hold values from 1000 to 1999
- block_count: int32 [16, 16], P('rows'), may hold values from 0 to 256, as said below
- time_freq: float32 [128], replicated, may hold values from 0.002 to 0.1
- time_phase: float32 [128], replicated, may hold values from -3.140625 to 3.140625
- w_pair: bfloat16 [128, 2, 384], P('cols'), may hold values from -0.3125 to 0.3125
- w_time: bfloat16 [128, 384], P('cols'), may hold values from -0.3125 to 0.3125
- w_hidden: bfloat16 [128, 384], P('cols'), may hold values from -0.5 to 0.5
- bias_input: float32 [384], P('cols'), may hold values from -3 to 3
- bias_hidden: float32 [384], P('cols'), may hold values from -3 to 3
Outputs:
- new_memory: float32 [128, 524288], P('cols', 'rows')
The draws below stay inside these ranges and needn't reach their ends.
Inputs may be any that keep to these rules, and one draw needn't show every extreme that they name: `slot_node`: every slot of block b (live or not) names a node of owner b, from b * 32768 to (b + 1) * 32768 - 1. `slot_pair`: indexes the holder's 16 * 256 slots flattened block by block; the relation is symmetric without fixed points, and live slots pair with live slots. `block_count`: every count is even; in every draw one owner's block is full (256 live slots) from every holder.
All inputs are finite; a program needn't handle non-finite values.
Results may differ from the reference program's by a relative error of at most 0.0006.
Values may be sent and summed in bfloat16 or wider, within the bound.
No kernel may reach another device: no remote copies, remote signals or barrier semaphores. Data moves between devices by JAX's collectives and lax.ppermute only.
A program may use at most 128 MiB of HBM per device.

```python
import math
import jax
import jax.numpy as jnp
from jax import lax

MEM = 128
TDIM = 128
NODE_DEV = 32768
CAP = 256
TICK_SPAN = 1000
NODES = 524288
N_ROWS = 16


def layout_all(key):
    base_key = jax.random.fold_in(key, 7)
    hot_key, count_key, node_key, order_key = jax.random.split(base_key, 4)
    hottest = jax.random.randint(hot_key, (), 0, N_ROWS)
    drawn = 2 * jax.random.randint(count_key, (N_ROWS, N_ROWS), CAP // 16, 5 * CAP // 32 + 1)
    counts = jnp.where(jnp.arange(N_ROWS)[None, :] == hottest, CAP, drawn).astype(jnp.int32)
    local = jax.random.randint(node_key, (N_ROWS, N_ROWS, CAP), 0, NODE_DEV)
    nodes = (jnp.arange(N_ROWS)[None, :, None] * NODE_DEV + local).astype(jnp.int32)
    span = N_ROWS * CAP
    filled = (jnp.arange(CAP)[None, None, :] < counts[:, :, None]).reshape(N_ROWS, span)
    ranks = jax.vmap(lambda k: jax.random.permutation(k, span))(jax.random.split(order_key, N_ROWS))
    score = jnp.where(filled, 0, span) + ranks
    order = jnp.argsort(score, axis=1, stable=True).astype(jnp.int32)
    flipped = jnp.arange(span) ^ 1

    def pair_row(row_order):
        return jnp.zeros((span,), jnp.int32).at[row_order].set(row_order[flipped])
    pairs = jax.vmap(pair_row)(order)
    return (counts, nodes.reshape(N_ROWS * N_ROWS, CAP), pairs.reshape(N_ROWS * N_ROWS, CAP))


def draw_block_count(key, part):
    return layout_all(key)[0]


def draw_slot_node(key, part):
    return layout_all(key)[1]


def draw_slot_pair(key, part):
    return layout_all(key)[2]


def set_ends(values, stream_key, low, high):
    longest = values.shape.index(max(values.shape))
    spots = []
    for shift in (0, 1):
        where = [jax.random.randint(jax.random.fold_in(stream_key, axis), (), 0, length) for axis, length in enumerate(values.shape)]
        where[longest] = (where[longest] + shift) % values.shape[longest]
        spots.append(tuple(where))
    return values.at[spots[0]].set(low).at[spots[1]].set(high)


def block_scale(rng, shape, pieces, low, largest):
    loudness = 1.0
    for position, shards_of in pieces:
        heights = jax.random.uniform(jax.random.fold_in(jax.random.fold_in(rng, 6), position), (shards_of,), jnp.float32, low / len(pieces), largest / len(pieces))
        loudness = loudness * jnp.repeat(jnp.exp(heights), shape[position] // shards_of).reshape((-1,) + (1,) * (len(shape) - 1 - position))
    return loudness


def centred(key, shape, scale, most, cuts=(), kind=jnp.bfloat16):
    level = block_scale(key, shape, cuts, -0.22, 0.18) if cuts else 1.0
    drawn = jax.random.normal(key, shape, jnp.float32) * scale * level
    return jnp.minimum(jnp.maximum(drawn, -most), most).astype(kind)


def setup_inputs(seed: int = 0) -> dict:
    keys = jax.random.split(jax.random.key(seed), 14)
    return {
        "memory": centred(keys[0], (MEM, NODES), 0.5, 3.0, ((0, 8), (1, 16)), jnp.float32),
        "last_tick": set_ends(jax.random.randint(keys[1], (NODES,), 0, TICK_SPAN), jax.random.fold_in(keys[1], 1), 0, TICK_SPAN - 1).astype(jnp.int32),
        "slot_node": draw_slot_node(jax.random.fold_in(keys[13], 71), 0),
        "slot_pair": draw_slot_pair(jax.random.fold_in(keys[13], 71), 0),
        "slot_tick": set_ends(jax.random.randint(keys[4], (N_ROWS * N_ROWS, CAP), TICK_SPAN, 2 * TICK_SPAN), jax.random.fold_in(keys[4], 1), TICK_SPAN, (2 * TICK_SPAN) - 1).astype(jnp.int32),
        "block_count": draw_block_count(jax.random.fold_in(keys[13], 71), 0),
        "time_freq": jnp.clip(jnp.exp(jax.random.uniform(keys[6], (TDIM,), jnp.float32, math.log(0.002), math.log(0.1))), 0.002, 0.1),
        "time_phase": jnp.clip(jax.random.uniform(keys[7], (TDIM,), jnp.float32, -3.140625, 3.140625), -3.140625, 3.140625),
        "w_pair": centred(keys[8], (MEM, 2, 3 * MEM), (2 * MEM + TDIM) ** -0.5, 0.3125, ((0, 8),)),
        "w_time": centred(keys[9], (TDIM, 3 * MEM), (2 * MEM + TDIM) ** -0.5, 0.3125, ((0, 8),)),
        "w_hidden": centred(keys[10], (MEM, 3 * MEM), MEM ** -0.5, 0.5, ((0, 8),)),
        "bias_input": centred(keys[11], (3 * MEM,), 0.5, 3.0, ((0, 8),), jnp.float32),
        "bias_hidden": centred(keys[12], (3 * MEM,), 0.5, 3.0, ((0, 8),), jnp.float32),
    }


def reference(memory, last_tick, slot_node, slot_pair, slot_tick, block_count, time_freq, time_phase, w_pair, w_time, w_hidden, bias_input, bias_hidden):
    width = memory.shape[0]
    slots = slot_node.reshape(N_ROWS, N_ROWS, CAP)
    flat_nodes = slot_node.reshape(N_ROWS, N_ROWS * CAP)
    partners = jnp.take_along_axis(flat_nodes, slot_pair.reshape(N_ROWS, N_ROWS * CAP), axis=1).reshape(N_ROWS, N_ROWS, CAP)
    ticks = slot_tick.reshape(N_ROWS, N_ROWS, CAP)
    filled = jnp.arange(CAP, dtype=jnp.int32)[None, None, :] < block_count[:, :, None]

    def owner_block(owner):
        nodes = slots[:, owner].reshape(-1)
        others = partners[:, owner].reshape(-1)
        live = filled[:, owner].reshape(-1)
        hidden = memory[:, nodes].T
        self_in = hidden.astype(jnp.bfloat16)
        partner_in = memory[:, others].T.astype(jnp.bfloat16)
        gaps = (ticks[:, owner].reshape(-1) - last_tick[nodes]).astype(jnp.float32)
        encoded = jnp.cos(gaps[:, None] * time_freq[None, :] + time_phase[None, :]).astype(jnp.bfloat16)
        gate_in = jnp.dot(self_in, w_pair[:, 0, :], preferred_element_type=jnp.float32)
        gate_in = gate_in + jnp.dot(partner_in, w_pair[:, 1, :], preferred_element_type=jnp.float32)
        gate_in = gate_in + jnp.dot(encoded, w_time, preferred_element_type=jnp.float32)
        gate_hid = jnp.dot(self_in, w_hidden, preferred_element_type=jnp.float32)
        local = jnp.where(live, nodes - owner * NODE_DEV, NODE_DEV).astype(jnp.int32)
        sums = jnp.zeros((NODE_DEV + 1, 3 * width), jnp.float32).at[local].add(gate_in)
        counts = jnp.zeros((NODE_DEV + 1,), jnp.float32).at[NODE_DEV].set(1.0).at[local].add(1.0)
        mean = sums[local] / counts[local][:, None]
        gx = (mean + bias_input[None, :]).reshape(-1, width, 3)
        gh = (gate_hid + bias_hidden[None, :]).reshape(-1, width, 3)
        reset = jax.nn.sigmoid(gx[:, :, 0] + gh[:, :, 0])
        keep = jax.nn.sigmoid(gx[:, :, 1] + gh[:, :, 1])
        cand = jnp.tanh(gx[:, :, 2] + reset * gh[:, :, 2])
        fresh = (1.0 - keep) * cand + keep * hidden
        block = lax.dynamic_slice_in_dim(memory, owner * NODE_DEV, NODE_DEV, 1)
        return block.at[:, local].set(fresh.T, mode="drop")

    result = lax.map(owner_block, jnp.arange(N_ROWS, dtype=jnp.int32))
    return jnp.transpose(result, (1, 0, 2)).reshape(width, N_ROWS * NODE_DEV)
```

```python
import jax
import jax.numpy as jnp
from jax import lax
from jax.experimental import pallas as pl
from jax.experimental.pallas import tpu as pltpu
from jax.sharding import PartitionSpec as P

BF = jnp.bfloat16
F32 = jnp.float32
I32 = jnp.int32
CAP = 256
SPAN = 1024
VMEM_BYTES = 48 << 20
SMEM = pl.BlockSpec(memory_space=pltpu.SMEM)
VMEM = pl.BlockSpec(memory_space=pltpu.VMEM)
HBM = pl.BlockSpec(memory_space=pltpu.MemorySpace.HBM)


def call(kernel, out_shape, specs, args, scratch=(), cost=None):
    outs = jax.tree.map(lambda _: VMEM, out_shape)
    return pl.pallas_call(
        kernel,
        out_shape=out_shape,
        in_specs=specs,
        out_specs=outs,
        scratch_shapes=list(scratch),
        compiler_params=pltpu.CompilerParams(vmem_limit_bytes=VMEM_BYTES),
        cost_estimate=cost,
    )(*args)


def cost(us):
    return pl.CostEstimate(flops=int(us * 1e8), bytes_accessed=int(us * 3.5e6), transcendentals=0)


def match(index, rows):
    places = lax.broadcasted_iota(I32, (rows, index.shape[1]), 0).astype(BF)
    return jnp.where(places == index.astype(BF), jnp.ones((), BF), jnp.zeros((), BF))


def match_wide(index, rows):
    parts = [
        match(jnp.where((index >> 8) == k, index & 255, -1), 256) for k in range(rows // 256)
    ]
    return jnp.concatenate(parts, axis=0)


def groups(index, values, count):
    low = index.astype(BF)
    rows = values.shape[0]
    zero = jnp.zeros((), BF)
    return jnp.concatenate(
        [jnp.where(low == jnp.full((rows, 1), k, BF), values, zero) for k in range(count)], axis=0
    )


def dot(a, b):
    return jnp.dot(a, b, preferred_element_type=F32)


def dot_nt(a, b):
    return lax.dot_general(a, b, (((1,), (1,)), ((), ())), preferred_element_type=F32)


def fetch(sems, *pairs):
    copies = [pltpu.make_async_copy(a, b, sems.at[k]) for k, (a, b) in enumerate(pairs)]
    for c in copies:
        c.start()
    for c in copies:
        c.wait()


def send_kernel(count_hbm, node_hbm, tick_hbm, out_ref, count_ref, node_ref, tick_ref, sems, *, nodes):
    fetch(sems, (count_hbm, count_ref), (node_hbm, node_ref), (tick_hbm, tick_ref))
    for b in range(node_ref.shape[0]):
        place = lax.broadcasted_iota(I32, (1, CAP), 1)
        ids = jnp.where(place < count_ref[0, b], node_ref[b : b + 1, :] - b * nodes, nodes)
        out_ref[b, 0:1, :] = ids
        out_ref[b, 1:2, :] = tick_ref[b : b + 1, :]


def prep_kernel(mem_hbm, wp_hbm, wt_hbm, wh_hbm, high_ref, low_ref, w_ref,
                mem_ref, wp_ref, wt_ref, wh_ref, sems):
    fetch(sems, (mem_hbm, mem_ref), (wp_hbm, wp_ref), (wt_hbm, wt_ref), (wh_hbm, wh_ref))
    feats = mem_ref.shape[0]
    for g in range(mem_ref.shape[1] // SPAN):
        x = mem_ref[:, g * SPAN : (g + 1) * SPAN]
        high = x.astype(BF)
        high_ref[g * feats : (g + 1) * feats, :] = high
        low_ref[g * feats : (g + 1) * feats, :] = (x - high.astype(F32)).astype(BF)
    for m, w in enumerate((wp_ref[:, 0, :], wp_ref[:, 1, :], wt_ref[...], wh_ref[...])):
        w_ref[m] = w[:, 0:256]
        w_ref[4 + m // 2, :, (m % 2) * 128 : (m % 2 + 1) * 128] = w[:, 256:384]


def gather_kernel(ids_ref, table_ref, out_ref):
    feats = out_ref.shape[1]
    count = table_ref.shape[0] // feats

    def body(h, carry):
        ids = ids_ref[h, 0:1, :]
        high = ids >> 10
        picked = dot(table_ref[...], match_wide(ids & (SPAN - 1), SPAN))
        total = jnp.zeros((feats, CAP), F32)
        for g in range(count):
            total = total + jnp.where(high == g, picked[g * feats : (g + 1) * feats, :], 0.0)
        out_ref[h] = total.astype(BF)
        return carry

    lax.fori_loop(0, ids_ref.shape[0], body, 0, unroll=4)


def rank_kernel(ids_ref, own_ref, w_ref, rank_ref, node_ref, inv_ref, self_ref, hi_s, lo_s, left_s, right_s):
    blocks = ids_ref.shape[0]
    feats = own_ref.shape[1]
    for h in range(blocks):
        ids = ids_ref[h, 0:1, :]
        at = slice(h * CAP, (h + 1) * CAP)
        hi_s[:, at] = match(ids >> 8, 128)
        lo_s[:, at] = match(ids & 255, 256)
    held = dot_nt(hi_s[...], lo_s[...])
    coarse = jnp.floor(held * (1.0 / 64.0))
    fine = (held - 64.0 * coarse).astype(BF)
    coarse = coarse.astype(BF)
    row, col = (lax.broadcasted_iota(I32, (256, 256), d) for d in (0, 1))
    before = jnp.where(row < col, 1.0, 0.0).astype(BF)
    inside = 64.0 * dot(coarse, before) + dot(fine, before)
    row, col = (lax.broadcasted_iota(I32, (128, 128), d) for d in (0, 1))
    above = jnp.where(col < row, 1.0, 0.0).astype(BF)
    ahead = 64.0 * dot(above, coarse) + dot(above, fine)
    ranks = inside + jnp.sum(ahead, axis=1, keepdims=True)
    coarse = jnp.floor(ranks * (1.0 / 64.0))
    fine = (ranks - 64.0 * coarse).astype(BF)
    table = jnp.concatenate([coarse.astype(BF), fine], axis=0)
    for h in range(blocks):
        ids = ids_ref[h, 0:1, :]
        at = slice(h * CAP, (h + 1) * CAP)
        picked = dot(table, lo_s[:, at])
        both = (64.0 * picked[:128] + picked[128:]) * hi_s[:, at].astype(F32)
        rank = jnp.sum(both, axis=0, keepdims=True).astype(I32)
        rank = jnp.where(ids < 32768, rank, blocks * CAP)
        rank_ref[h] = rank
        extra = jnp.concatenate(
            [
                jnp.ones((1, CAP), F32),
                (ids >> 8).astype(F32),
                (ids & 255).astype(F32),
                jnp.zeros((13, CAP), F32),
            ],
            axis=0,
        ).astype(BF)
        values = jnp.concatenate([own_ref[h], extra], axis=0)
        left_s[:, at] = groups(rank >> 8, values, blocks)
        right_s[:, at] = match(rank & 255, 256)
    sums = dot_nt(left_s[...], right_s[...])
    step = feats + 16
    for a in range(blocks):
        n = sums[a * step + feats : a * step + feats + 1]
        inv = 1.0 / jnp.maximum(n, 1.0)
        high = sums[a * step + feats + 1 : a * step + feats + 2] * inv + 0.5
        low = sums[a * step + feats + 2 : a * step + feats + 3] * inv + 0.5
        node = (high.astype(I32) << 8) + low.astype(I32)
        node_ref[a] = jnp.where(n > 0.0, node, 32768)
        inv_ref[a] = inv
        self_ref[a] = (sums[a * step : a * step + feats] * inv).astype(BF)
    self_ref[blocks:] = w_ref[...]


def permute_kernel(pair_ref, rows_ref, out_ref):
    blocks, feats, _ = rows_ref.shape
    table = rows_ref[...].reshape(blocks * feats, CAP)
    for b in range(blocks):
        pair = pair_ref[b : b + 1, :]
        high = pair >> 8
        picked = dot(table, match(pair & 255, 256))
        total = jnp.zeros((feats, CAP), F32)
        for g in range(blocks):
            total = total + jnp.where(high == g, picked[g * feats : (g + 1) * feats, :], 0.0)
        out_ref[b] = total.astype(BF)


def mean_kernel(rank_ref, inv_ref, rows_ref, out_ref, left_s, right_s):
    blocks, feats, _ = rows_ref.shape
    for h in range(blocks):
        rank = rank_ref[h]
        at = slice(h * CAP, (h + 1) * CAP)
        left_s[:, at] = groups(rank >> 8, rows_ref[h], blocks)
        right_s[:, at] = match(rank & 255, 256)
    sums = dot_nt(left_s[...], right_s[...])
    for a in range(blocks):
        out_ref[a] = (sums[a * feats : (a + 1) * feats] * inv_ref[a]).astype(BF)


def weights_kernel(order_ref, *refs):
    pieces, (bi_ref, bh_ref, out_ref, bias_ref, all_s) = refs[:8], refs[8:]
    column = order_ref[8]
    feats = 16
    for k, piece in enumerate(pieces):
        for m in range(4):
            at = (slice(m * feats, (m + 1) * feats), slice(0, 256))
            all_s[(k, *at)] = piece[16 + m]
            at = (slice(m * feats, (m + 1) * feats), slice(256, 384))
            all_s[(k, *at)] = piece[20 + m // 2, :, (m % 2) * 128 : (m % 2 + 1) * 128]
    out_row = lax.broadcasted_iota(I32, (48, 384), 0)
    source = lax.broadcasted_iota(I32, (48, 384), 1)
    wanted = 48 * column + 3 * (out_row & 15) + (out_row >> 4)
    pick = jnp.where(source == wanted, 1.0, 0.0).astype(BF)
    for m in range(4):
        rows = [
            all_s[order_ref[k] if m == 2 else k, m * feats : (m + 1) * feats, :] for k in range(8)
        ]
        out_ref[m] = dot_nt(pick, jnp.concatenate(rows, axis=0)).astype(BF)
    out_row = lax.broadcasted_iota(I32, (48, 48), 0)
    source = lax.broadcasted_iota(I32, (48, 48), 1)
    same = source == 3 * (out_row & 15) + (out_row >> 4)
    for k, ref in enumerate((bi_ref, bh_ref)):
        column_of = jnp.sum(jnp.where(same, ref[...], 0.0), axis=1, keepdims=True)
        bias_ref[k] = jnp.broadcast_to(column_of, (48, 128))


def cosine(x):
    turns = jnp.floor(x * 0.15915494309189535 + 0.5)
    u = 0.5 * x - turns * 3.140625
    u = u - turns * 9.67653589793e-4
    s = u * u
    q = s * -2.50521084e-08 + 2.75573192e-06
    q = q * s - 1.98412698e-04
    q = q * s + 8.33333333e-03
    q = q * s - 1.66666667e-01
    sine = u + u * s * q
    return 1.0 - 2.0 * sine * sine


def time_kernel(ids_ref, last_ref, freq_ref, phase_ref, w_ref, rank_ref, inv_ref, out_ref,
                table_s, left_s, right_s, acc_s):
    blocks = ids_ref.shape[0]
    gates = out_ref.shape[1]
    for k in range(8):
        last = last_ref[pl.ds(k, 32, stride=8), :]
        table_s[0:32, k * 128 : (k + 1) * 128] = (last >> 3).astype(F32).astype(BF)
        table_s[32:64, k * 128 : (k + 1) * 128] = (last & 7).astype(F32).astype(BF)
    freq = jnp.transpose(jnp.broadcast_to(freq_ref[...], (128, 128)))[:, 0:1]
    phase = jnp.transpose(jnp.broadcast_to(phase_ref[...], (128, 128)))[:, 0:1]
    acc_s[...] = jnp.zeros_like(acc_s)

    def body(q, carry):
        for i in range(4):
            h = q * 4 + i
            ids = ids_ref[h, 0:1, :]
            picked = dot(table_s[...], match_wide(ids & (SPAN - 1), SPAN))
            row = lax.broadcasted_iota(I32, (32, CAP), 0)
            last = jnp.sum(
                jnp.where(row == (ids >> 10), 8.0 * picked[:32] + picked[32:], 0.0),
                axis=0,
                keepdims=True,
            )
            gap = ids_ref[h, 1:2, :].astype(F32) - last
            encoded = cosine(gap * freq + phase).astype(BF)
            part = dot(w_ref[2], encoded)
            high = part.astype(BF)
            low = (part - high.astype(F32)).astype(BF)
            rank = rank_ref[h]
            at = slice(i * CAP, (i + 1) * CAP)
            left_s[:, at] = groups(rank >> 8, jnp.concatenate([high, low], axis=0), blocks)
            right_s[:, at] = match(rank & 255, 256)
        acc_s[...] += dot_nt(left_s[...], right_s[...])
        return carry

    lax.fori_loop(0, blocks // 4, body, 0)
    for a in range(blocks):
        both = acc_s[2 * gates * a : 2 * gates * (a + 1), :]
        out_ref[a] = (both[:gates] + both[gates:]) * inv_ref[a]


def self_kernel(*refs):
    pieces, (w_ref, bias_ref, time_ref, out_ref) = refs[:8], refs[8:]

    def body(a, carry):
        full = jnp.concatenate([p[a] for p in pieces], axis=0)
        out_ref[a, 0:48] = dot(w_ref[0], full) + time_ref[a] + bias_ref[0, :, 0:1]
        out_ref[a, 48:96] = dot(w_ref[3], full) + bias_ref[1, :, 0:1]
        return carry

    lax.fori_loop(0, out_ref.shape[0], body, 0, unroll=4)


def final_kernel(*refs):
    pieces = refs[:8]
    w_ref, pre_ref, high_ref, low_ref, node_ref, mem_hbm, out_ref = refs[8:15]
    mem_ref, change_s, acc_s, sem = refs[15:]
    load = pltpu.make_async_copy(mem_hbm, mem_ref, sem)
    load.start()
    blocks, feats, _ = low_ref.shape
    count = mem_ref.shape[1] // SPAN
    acc_s[...] = jnp.zeros_like(acc_s)

    def gates(a, carry):
        full = jnp.concatenate([p[a] for p in pieces], axis=0)
        gx = pre_ref[a, 0:48] + dot(w_ref[1], full)
        gh = pre_ref[a, 48:96]
        reset = jax.nn.sigmoid(gx[0:16] + gh[0:16])
        keep = jax.nn.sigmoid(gx[16:32] + gh[16:32])
        cand = jnp.tanh(gx[32:48] + reset * gh[32:48])
        hidden = high_ref[a].astype(F32) + low_ref[a].astype(F32)
        change = (1.0 - keep) * (cand - hidden)
        high = change.astype(BF)
        change_s[a, 0:feats] = high
        change_s[a, feats : 2 * feats] = (change - high.astype(F32)).astype(BF)
        return carry

    lax.fori_loop(0, blocks, gates, 0, unroll=4)

    def scatter(a, carry):
        node = node_ref[a]
        spread = match_wide(node & (SPAN - 1), SPAN)
        group = node >> 10
        acc = dot_nt(groups(group, change_s[a, 0:feats], count), spread)
        acc = acc + dot_nt(groups(group, change_s[a, feats : 2 * feats], count), spread)
        acc_s[...] += acc
        return carry

    lax.fori_loop(0, blocks, scatter, 0, unroll=4)
    load.wait()
    for g in range(count):
        at = slice(g * SPAN, (g + 1) * SPAN)
        out_ref[:, at] = mem_ref[:, at] + acc_s[g * feats : (g + 1) * feats, :]


def shape(s, d):
    return jax.ShapeDtypeStruct(s, d)


def local(
    memory,
    last_tick,
    slot_node,
    slot_pair,
    slot_tick,
    block_count,
    time_freq,
    time_phase,
    w_pair,
    w_time,
    w_hidden,
    bias_input,
    bias_hidden,
):
    feats, nodes = memory.shape
    blocks, cap = slot_node.shape
    total = blocks * cap
    tile = (blocks, feats, cap)
    column = lax.axis_index("cols").astype(I32)

    def from_columns(x):
        same = [x]
        for d in (1, 2, 3):
            same.append(
                lax.ppermute(x, "cols", [(j, ((j // 2 + d) % 4) * 2 + j % 2) for j in range(8)])
            )
        return same + [lax.ppermute(p, "cols", [(j, j ^ 1) for j in range(8)]) for p in same]

    def swap(x):
        return lax.all_to_all(x, "rows", split_axis=0, concat_axis=0, tiled=True)

    sems = pltpu.SemaphoreType.DMA
    asked = call(
        lambda *r: send_kernel(*r, nodes=nodes),
        shape((blocks, 2, cap), I32),
        [HBM] * 3,
        (block_count, slot_node, slot_tick),
        scratch=(
            pltpu.SMEM((1, blocks), I32),
            pltpu.VMEM((blocks, cap), I32),
            pltpu.VMEM((blocks, cap), I32),
            sems((3,)),
        ),
        cost=cost(2),
    )
    asked = swap(asked)
    groups_of = nodes // SPAN
    table = shape((groups_of * feats, SPAN), BF)
    high, low, packed = call(
        prep_kernel,
        (table, table, shape((6, feats, cap), BF)),
        [HBM] * 4,
        (memory, w_pair, w_time, w_hidden),
        scratch=(
            pltpu.VMEM((feats, nodes), F32),
            pltpu.VMEM(w_pair.shape, BF),
            pltpu.VMEM(w_time.shape, BF),
            pltpu.VMEM(w_hidden.shape, BF),
            sems((4,)),
        ),
        cost=cost(3),
    )
    own = call(gather_kernel, shape(tile, BF), [VMEM] * 2, (asked, high), cost=cost(7))
    held = swap(own)
    rank, node, inv, self_rows = call(
        rank_kernel,
        (
            shape((blocks, 1, cap), I32),
            shape((blocks, 1, cap), I32),
            shape((blocks, 1, cap), F32),
            shape((blocks + 6, feats, cap), BF),
        ),
        [VMEM] * 3,
        (asked, own, packed),
        scratch=(
            pltpu.VMEM((128, total), BF),
            pltpu.VMEM((256, total), BF),
            pltpu.VMEM((blocks * (feats + 16), total), BF),
            pltpu.VMEM((256, total), BF),
        ),
        cost=cost(5),
    )
    self_full = from_columns(self_rows)
    partner = call(permute_kernel, shape(tile, BF), [VMEM] * 2, (slot_pair, held), cost=cost(2))
    arrived = swap(partner)
    z, side = column >> 1, column & 1
    each = jnp.arange(8, dtype=I32)
    order = ((z - (each >> 1)) & 3) + 4 * ((each & 1) ^ side)
    order = jnp.concatenate([order, column[None]])
    wide, bias = call(
        weights_kernel,
        (shape((4, 48, 128), BF), shape((2, 48, 128), F32)),
        [SMEM] + [VMEM] * 10,
        (
            order,
            *self_full,
            bias_input.reshape(1, 48),
            bias_hidden.reshape(1, 48),
        ),
        scratch=(pltpu.VMEM((8, 4 * feats, 384), BF),),
        cost=cost(2),
    )
    timed = call(
        time_kernel,
        shape((blocks, 48, cap), F32),
        [VMEM] * 7,
        (
            asked,
            last_tick.reshape(nodes // 128, 128),
            time_freq.reshape(1, 128),
            time_phase.reshape(1, 128),
            wide,
            rank,
            inv,
        ),
        scratch=(
            pltpu.VMEM((2 * groups_of, SPAN), BF),
            pltpu.VMEM((blocks * 96, 4 * cap), BF),
            pltpu.VMEM((256, 4 * cap), BF),
            pltpu.VMEM((blocks * 96, 256), F32),
        ),
        cost=cost(10),
    )
    rest = call(gather_kernel, shape(tile, BF), [VMEM] * 2, (node, low), cost=cost(7))
    mean = call(
        mean_kernel,
        shape(tile, BF),
        [VMEM] * 3,
        (rank, inv, arrived),
        scratch=(pltpu.VMEM((256, total), BF), pltpu.VMEM((256, total), BF)),
        cost=cost(2),
    )
    partners = from_columns(mean)
    pre = call(
        self_kernel,
        shape((blocks, 96, cap), F32),
        [VMEM] * 11,
        (*self_full, wide, bias, timed),
        cost=cost(2),
    )
    return call(
        final_kernel,
        shape((feats, nodes), F32),
        [VMEM] * 13 + [HBM],
        (*partners, wide, pre, self_rows, rest, node, memory),
        scratch=(
            pltpu.VMEM((feats, nodes), F32),
            pltpu.VMEM((blocks, 2 * feats, cap), BF),
            pltpu.VMEM((groups_of * feats, SPAN), F32),
            sems(()),
        ),
        cost=cost(14),
    )


def solution(mesh):
    placed = (
        P("cols", "rows"),
        P("rows"),
        P("rows", None),
        P("rows", None),
        P("rows", None),
        P("rows", None),
        P(),
        P(),
        P("cols", None, None),
        P("cols", None),
        P("cols", None),
        P("cols"),
        P("cols"),
    )
    return jax.shard_map(
        local, mesh=mesh, in_specs=placed, out_specs=P("cols", "rows"), check_vma=False
    )
```

```python
import jax
import jax.numpy as jnp
from jax import lax
from jax.experimental import pallas as pl
from jax.experimental.pallas import tpu as pltpu
from jax.sharding import PartitionSpec as P

BF = jnp.bfloat16
F32 = jnp.float32
I32 = jnp.int32
CAP = 256
SPAN = 1024
WINDOW = 12
VMEM_BYTES = 24 << 20
SCALE = 1.0
SMEM = pl.BlockSpec(memory_space=pltpu.SMEM)
VMEM = pl.BlockSpec(memory_space=pltpu.VMEM)
ANY = pl.BlockSpec(memory_space=pl.ANY)
HBM = pl.BlockSpec(memory_space=pltpu.MemorySpace.HBM)


def call(
    kernel, out_shape, specs, args, scratch=(), cost=None, after=(), vmem=VMEM_BYTES, outs=None
):
    def body(*refs):
        kernel(*refs[len(after) :])

    outs = outs or jax.tree.map(lambda _: VMEM, out_shape)
    return pl.pallas_call(
        body,
        out_shape=out_shape,
        in_specs=[ANY] * len(after) + list(specs),
        out_specs=outs,
        scratch_shapes=list(scratch),
        compiler_params=pltpu.CompilerParams(vmem_limit_bytes=vmem),
        cost_estimate=cost,
    )(*after, *args)


def cost(us):
    return pl.CostEstimate(flops=int(us * SCALE * 1e8), bytes_accessed=int(us * SCALE * 3.5e6), transcendentals=0)


def match(index, rows):
    places = lax.broadcasted_iota(I32, (rows, index.shape[1]), 0).astype(BF)
    return jnp.where(places == index.astype(BF), jnp.ones((), BF), jnp.zeros((), BF))


def match_wide(index, rows):
    parts = [
        match(jnp.where((index >> 8) == k, index & 255, -1), 256) for k in range(rows // 256)
    ]
    return jnp.concatenate(parts, axis=0)


def groups(index, values, count):
    low = index.astype(BF)
    rows = values.shape[0]
    zero = jnp.zeros((), BF)
    return jnp.concatenate(
        [jnp.where(low == jnp.full((rows, 1), k, BF), values, zero) for k in range(count)], axis=0
    )


def dot(a, b):
    return jnp.dot(a, b, preferred_element_type=F32)


def dot_nt(a, b):
    return lax.dot_general(a, b, (((1,), (1,)), ((), ())), preferred_element_type=F32)


def fetch(sems, *pairs):
    copies = [pltpu.make_async_copy(a, b, sems.at[k]) for k, (a, b) in enumerate(pairs)]
    for c in copies:
        c.start()
    for c in copies:
        c.wait()


def rank_of(info, h):
    return info[h, 0:1, :].astype(I32)


def inv_of(info, a):
    return info[a, 1:2, :]


def gap_of(info, h):
    return info[h, 2:3, :]


def node_of(info, a):
    return info[a, 3:4, :].astype(I32)


def send_kernel(count_hbm, node_hbm, tick_hbm, out_ref, count_ref, node_ref, tick_ref, sems, *, nodes):
    fetch(sems, (count_hbm, count_ref), (node_hbm, node_ref), (tick_hbm, tick_ref))
    for b in range(node_ref.shape[0]):
        place = lax.broadcasted_iota(I32, (1, CAP), 1)
        ids = jnp.where(place < count_ref[0, b], node_ref[b : b + 1, :] - b * nodes, nodes)
        out_ref[b, 0:1, :] = ids
        out_ref[b, 1:2, :] = tick_ref[b : b + 1, :]


def prep_kernel(mem_ref, high_ref, low_ref):
    feats = mem_ref.shape[0]
    for g in range(mem_ref.shape[1] // SPAN):
        x = mem_ref[:, g * SPAN : (g + 1) * SPAN]
        high = x.astype(BF)
        high_ref[g * feats : (g + 1) * feats, :] = high
        low_ref[g * feats : (g + 1) * feats, :] = (x - high.astype(F32)).astype(BF)


def gather_kernel(ids_ref, table_ref, out_ref):
    feats = out_ref.shape[1]
    count = table_ref.shape[0] // feats

    def body(h, carry):
        ids = ids_ref[h, 0:1, :]
        high = ids >> 10
        picked = dot(table_ref[...], match_wide(ids & (SPAN - 1), SPAN))
        total = jnp.zeros((feats, CAP), F32)
        for g in range(count):
            total = total + jnp.where(high == g, picked[g * feats : (g + 1) * feats, :], 0.0)
        out_ref[h] = total.astype(BF)
        return carry

    lax.fori_loop(0, ids_ref.shape[0], body, 0, unroll=4)


def own_kernel(ids_ref, table_ref, wp_ref, wt_ref, wh_ref, out_ref, wide_ref):
    gather_kernel(ids_ref, table_ref, out_ref)
    at = out_ref.shape[0]
    wide_ref[0:at] = out_ref[...]
    for m, w in enumerate((wp_ref[:, 0, :], wp_ref[:, 1, :], wt_ref[...], wh_ref[...])):
        wide_ref[at + m] = w[:, 0:256]
        wide_ref[at + 4 + m // 2, :, (m % 2) * 128 : (m % 2 + 1) * 128] = w[:, 256:384]


def sorted_gather_kernel(info_ref, range_ref, table_ref, out_ref):
    feats = out_ref.shape[1]
    count = table_ref.shape[0] // feats

    def window(a, k):
        lowest = range_ref[0, a] + k * WINDOW
        start = jnp.minimum(lowest, count - WINDOW)
        node = node_of(info_ref, a)
        group = node >> 10
        place = jnp.where(group >= lowest, group - start, -1)
        rows = table_ref[pl.ds(pl.multiple_of(start * feats, feats), WINDOW * feats), :]
        picked = dot(rows, match_wide(node & (SPAN - 1), SPAN))
        total = jnp.zeros((feats, CAP), F32)
        for g in range(WINDOW):
            total = total + jnp.where(place == g, picked[g * feats : (g + 1) * feats, :], 0.0)
        return total.astype(BF)

    def first(a, carry):
        out_ref[a] = window(a, 0)
        return carry

    lax.fori_loop(0, out_ref.shape[0], first, 0, unroll=4)

    def others(a, carry):
        def one(k, c):
            out_ref[a] += window(a, k)
            return c

        lax.fori_loop(1, range_ref[1, a], one, 0)
        return carry

    lax.fori_loop(0, out_ref.shape[0], others, 0)


def rank_kernel(ids_ref, last_ref, info_ref, range_ref,
                hi_s, lo_s, left_s, right_s, table_s):
    blocks = ids_ref.shape[0]
    for h in range(blocks):
        ids = ids_ref[h, 0:1, :]
        at = slice(h * CAP, (h + 1) * CAP)
        hi_s[:, at] = match(ids >> 8, 128)
        lo_s[:, at] = match(ids & 255, 256)
    held = dot_nt(hi_s[...], lo_s[...])
    coarse = jnp.floor(held * (1.0 / 64.0))
    fine = (held - 64.0 * coarse).astype(BF)
    coarse = coarse.astype(BF)
    row, col = (lax.broadcasted_iota(I32, (256, 256), d) for d in (0, 1))
    before = jnp.where(row < col, 1.0, 0.0).astype(BF)
    inside = 64.0 * dot(coarse, before) + dot(fine, before)
    row, col = (lax.broadcasted_iota(I32, (128, 128), d) for d in (0, 1))
    above = jnp.where(col < row, 1.0, 0.0).astype(BF)
    ahead = 64.0 * dot(above, coarse) + dot(above, fine)
    ranks = inside + jnp.sum(ahead, axis=1, keepdims=True)
    coarse = jnp.floor(ranks * (1.0 / 64.0))
    fine = (ranks - 64.0 * coarse).astype(BF)
    table_s[0:128] = coarse.astype(BF)
    table_s[128:256] = fine
    for k in range(2):
        last = last_ref[pl.ds(k, 128, stride=2), :]
        at = slice(k * 128, (k + 1) * 128)
        table_s[256:384, at] = (last >> 3).astype(F32).astype(BF)
        table_s[384:512, at] = (last & 7).astype(F32).astype(BF)
    for h in range(blocks):
        ids = ids_ref[h, 0:1, :]
        at = slice(h * CAP, (h + 1) * CAP)
        picked = dot(table_s[...], lo_s[:, at])
        mask = hi_s[:, at].astype(F32)
        both = (64.0 * picked[0:128] + picked[128:256]) * mask
        rank = jnp.sum(both, axis=0, keepdims=True).astype(I32)
        both = (8.0 * picked[256:384] + picked[384:512]) * mask
        info_ref[h, 2:3, :] = ids_ref[h, 1:2, :].astype(F32) - jnp.sum(both, axis=0, keepdims=True)
        rank = jnp.where(ids < 32768, rank, blocks * CAP)
        info_ref[h, 0:1, :] = rank.astype(F32)
        values = jnp.concatenate(
            [
                jnp.ones((1, CAP), F32),
                (ids >> 8).astype(F32),
                (ids & 255).astype(F32),
                jnp.zeros((13, CAP), F32),
            ],
            axis=0,
        ).astype(BF)
        left_s[:, at] = groups(rank >> 8, values, blocks)
        right_s[:, at] = match(rank & 255, 256)
    sums = dot_nt(left_s[...], right_s[...])
    for a in range(blocks):
        n = sums[a * 16 : a * 16 + 1]
        inv = 1.0 / jnp.maximum(n, 1.0)
        high = sums[a * 16 + 1 : a * 16 + 2] * inv + 0.5
        low = sums[a * 16 + 2 : a * 16 + 3] * inv + 0.5
        node = (high.astype(I32) << 8) + low.astype(I32)
        info_ref[a, 1:2, :] = inv
        info_ref[a, 3:4, :] = jnp.where(n > 0.0, node, 32768).astype(F32)
        first = jnp.minimum(jnp.min(jnp.where(n > 0.0, node, 32768)) >> 10, 32 - WINDOW)
        last = jnp.max(jnp.where(n > 0.0, node, 0)) >> 10
        range_ref[0, a] = first
        range_ref[1, a] = 1 + jnp.maximum(last - first, 0) // WINDOW


def permute_kernel(pair_ref, rows_ref, out_ref):
    blocks, feats, _ = rows_ref.shape
    table = rows_ref[...].reshape(blocks * feats, CAP)
    for b in range(blocks):
        pair = pair_ref[b : b + 1, :]
        high = pair >> 8
        picked = dot(table, match(pair & 255, 256))
        total = jnp.zeros((feats, CAP), F32)
        for g in range(blocks):
            total = total + jnp.where(high == g, picked[g * feats : (g + 1) * feats, :], 0.0)
        out_ref[b] = total.astype(BF)


def mean_kernel(info_ref, rows_ref, out_ref, left_s, right_s):
    blocks, feats, _ = rows_ref.shape
    for h in range(blocks):
        rank = rank_of(info_ref, h)
        at = slice(h * CAP, (h + 1) * CAP)
        left_s[:, at] = groups(rank >> 8, rows_ref[h], blocks)
        right_s[:, at] = match(rank & 255, 256)
    sums = dot_nt(left_s[...], right_s[...])
    for a in range(blocks):
        out_ref[a] = (sums[a * feats : (a + 1) * feats] * inv_of(info_ref, a)).astype(BF)


def time_mean_kernel(info_ref, freq_ref, phase_ref, out_ref,
                     left_s, right_s, acc_s):
    blocks, feats, _ = out_ref.shape
    freq = jnp.transpose(jnp.broadcast_to(freq_ref[...], (128, 128)))[:, 0:1]
    phase = jnp.transpose(jnp.broadcast_to(phase_ref[...], (128, 128)))[:, 0:1]
    for q in range(4):
        for i in range(4):
            h = q * 4 + i
            encoded = cosine(gap_of(info_ref, h) * freq + phase).astype(BF)
            at = slice(i * CAP, (i + 1) * CAP)
            left_s[:, at] = groups(rank_of(info_ref, h) >> 8, encoded, blocks)
            right_s[:, at] = match(rank_of(info_ref, h) & 255, 256)
        sums = dot_nt(left_s[...], right_s[...])
        if q == 0:
            acc_s[...] = sums
        elif q < 3:
            acc_s[...] += sums
        else:
            for a in range(blocks):
                at = slice(feats * a, feats * (a + 1))
                out_ref[a] = ((acc_s[at] + sums[at]) * inv_of(info_ref, a)).astype(BF)


def eight(refs):
    return [r for k in (0, 2) for r in (refs[k], *[refs[k + 1].at[i] for i in range(3)])]


def weights_kernel(*refs):
    pieces, (bi_ref, bh_ref, out_ref, bias_ref, all_s) = eight(refs), refs[4:]
    column = lax.axis_index("cols")
    z, side = column >> 1, column & 1
    order = [((z - (k >> 1)) & 3) + 4 * ((k & 1) ^ side) for k in range(8)]
    feats = 16
    for k, piece in enumerate(pieces):
        for m in range(4):
            at = (slice(m * feats, (m + 1) * feats), slice(0, 256))
            all_s[(k, *at)] = piece[16 + m]
            at = (slice(m * feats, (m + 1) * feats), slice(256, 384))
            all_s[(k, *at)] = piece[20 + m // 2, :, (m % 2) * 128 : (m % 2 + 1) * 128]
    out_row = lax.broadcasted_iota(I32, (48, 384), 0)
    source = lax.broadcasted_iota(I32, (48, 384), 1)
    wanted = 48 * column + 3 * (out_row & 15) + (out_row >> 4)
    pick = jnp.where(source == wanted, 1.0, 0.0).astype(BF)
    for m in range(4):
        rows = [
            all_s[order[k] if m == 2 else k, m * feats : (m + 1) * feats, :] for k in range(8)
        ]
        out_ref[m] = dot_nt(pick, jnp.concatenate(rows, axis=0)).astype(BF)
    out_row = lax.broadcasted_iota(I32, (48, 48), 0)
    source = lax.broadcasted_iota(I32, (48, 48), 1)
    same = source == 3 * (out_row & 15) + (out_row >> 4)
    for k, ref in enumerate((bi_ref, bh_ref)):
        column_of = jnp.sum(jnp.where(same, ref[...], 0.0), axis=1, keepdims=True)
        bias_ref[k] = jnp.broadcast_to(column_of, (48, 128))


def cosine(x):
    turns = jnp.floor(x * 0.15915494309189535 + 0.5)
    u = 0.5 * x - turns * 3.140625
    u = u - turns * 9.67653589793e-4
    s = u * u
    q = s * -2.50521084e-08 + 2.75573192e-06
    q = q * s - 1.98412698e-04
    q = q * s + 8.33333333e-03
    q = q * s - 1.66666667e-01
    sine = u + u * s * q
    return 1.0 - 2.0 * sine * sine


def stack_kernel(p1, p2, p3, out_ref):
    for k, p in enumerate((p1, p2, p3)):
        out_ref[k] = p[...]


def self_kernel(*refs):
    pieces = eight(refs)
    info_ref, w_ref, bias_ref, code_ref, out_ref, own_ref = refs[4:10]
    left_s, right_s, acc_s = refs[10:]
    blocks, feats, _ = own_ref.shape
    rows = 8 * feats
    for q in range(4):
        for i in range(4):
            h = q * 4 + i
            full = jnp.concatenate([p[h] for p in pieces], axis=0)
            at = slice(i * CAP, (i + 1) * CAP)
            left_s[:, at] = groups(rank_of(info_ref, h) >> 8, full, blocks)
            right_s[:, at] = match(rank_of(info_ref, h) & 255, 256)
        sums = dot_nt(left_s[...], right_s[...])
        if q == 0:
            acc_s[...] = sums
        elif q < 3:
            acc_s[...] += sums
        else:
            for a in range(blocks):
                at = slice(rows * a, rows * (a + 1))
                full = ((acc_s[at] + sums[at]) * inv_of(info_ref, a)).astype(BF)
                own_ref[a] = full[0:feats]
                gx = dot(w_ref[0], full) + dot(w_ref[2], code_ref[a])
                out_ref[a, 0:48] = gx + bias_ref[0, :, 0:1]
                out_ref[a, 48:96] = dot(w_ref[3], full) + bias_ref[1, :, 0:1]


def final_kernel(*refs):
    pieces = eight(refs)
    w_ref, pre_ref, high_ref, low_ref, info_ref, range_ref, mem_hbm, out_ref = refs[4:12]
    mem_ref, change_s, acc_s, sem = refs[12:]
    load = pltpu.make_async_copy(mem_hbm, mem_ref, sem)
    load.start()
    blocks, feats, _ = low_ref.shape
    count = mem_ref.shape[1] // SPAN
    span = WINDOW * feats
    acc_s[...] = jnp.zeros_like(acc_s)

    def gates(a, carry):
        full = jnp.concatenate([p[a] for p in pieces], axis=0)
        gx = pre_ref[a, 0:48] + dot(w_ref[1], full)
        gh = pre_ref[a, 48:96]
        reset = jax.nn.sigmoid(gx[0:16] + gh[0:16])
        keep = jax.nn.sigmoid(gx[16:32] + gh[16:32])
        cand = jnp.tanh(gx[32:48] + reset * gh[32:48])
        hidden = high_ref[a].astype(F32) + low_ref[a].astype(F32)
        change = (1.0 - keep) * (cand - hidden)
        high = change.astype(BF)
        change_s[a, 0:feats] = high
        change_s[a, feats : 2 * feats] = (change - high.astype(F32)).astype(BF)
        return carry

    lax.fori_loop(0, blocks, gates, 0, unroll=4)

    def add_window(a, k):
        lowest = range_ref[0, a] + k * WINDOW
        start = jnp.minimum(lowest, count - WINDOW)
        node = node_of(info_ref, a)
        group = node >> 10
        place = jnp.where(group >= lowest, group - start, -1)
        spread = match_wide(node & (SPAN - 1), SPAN)
        left = [
            groups(place, change_s[a, f * feats : (f + 1) * feats], WINDOW) for f in range(2)
        ]
        sums = dot_nt(jnp.concatenate(left, axis=0), spread)
        at = pl.ds(pl.multiple_of(start * feats, feats), span)
        acc_s[at, :] += sums[:span] + sums[span:]

    def first_windows(a, carry):
        add_window(a, 0)
        return carry

    lax.fori_loop(0, blocks, first_windows, 0, unroll=4)

    def other_windows(a, carry):
        def one(k, c):
            add_window(a, k)
            return c

        lax.fori_loop(1, range_ref[1, a], one, 0)
        return carry

    lax.fori_loop(0, blocks, other_windows, 0)
    load.wait()
    for g in range(count):
        at = slice(g * SPAN, (g + 1) * SPAN)
        out_ref[:, at] = mem_ref[:, at] + acc_s[g * feats : (g + 1) * feats, :]


def shape(s, d):
    return jax.ShapeDtypeStruct(s, d)


def local(
    memory,
    last_tick,
    slot_node,
    slot_pair,
    slot_tick,
    block_count,
    time_freq,
    time_phase,
    w_pair,
    w_time,
    w_hidden,
    bias_input,
    bias_hidden,
):
    feats, nodes = memory.shape
    blocks, cap = slot_node.shape
    total = blocks * cap
    tile = (blocks, feats, cap)

    def along_z(x):
        return [
            lax.ppermute(x, "cols", [(j, ((j // 2 + d) % 4) * 2 + j % 2) for j in range(8)])
            for d in (1, 2, 3)
        ]

    def other_core(x):
        return lax.ppermute(x, "cols", [(j, j ^ 1) for j in range(8)])

    def swap(x):
        return lax.all_to_all(x, "rows", split_axis=0, concat_axis=0, tiled=True)

    sems = pltpu.SemaphoreType.DMA
    asked = call(
        lambda *r: send_kernel(*r, nodes=nodes),
        shape((blocks, 2, cap), I32),
        [HBM] * 3,
        (block_count, slot_node, slot_tick),
        scratch=(
            pltpu.SMEM((1, blocks), I32),
            pltpu.VMEM((blocks, cap), I32),
            pltpu.VMEM((blocks, cap), I32),
            sems((3,)),
        ),
        cost=cost(2),
        vmem=60 << 20,
    )
    groups_of = nodes // SPAN
    table = shape((groups_of * feats, SPAN), BF)
    high, low = call(
        prep_kernel, (table, table), [VMEM], (memory,), cost=cost(1), after=(asked,)
    )
    asked = swap(asked)
    own, own_wide = call(
        own_kernel,
        (shape(tile, BF), shape((blocks + 6, feats, cap), BF)),
        [VMEM] * 5,
        (asked, high, w_pair, w_time, w_hidden),
        cost=cost(7),
    )
    own_around = along_z(own_wide)
    held = swap(own)
    info, ranges = call(
        rank_kernel,
        (
            shape((blocks, 4, cap), F32),
            shape((2, blocks), I32),
        ),
        [VMEM] * 2,
        (asked, last_tick.reshape(nodes // 128, 128)),
        scratch=(
            pltpu.VMEM((128, total), BF),
            pltpu.VMEM((256, total), BF),
            pltpu.VMEM((256, total), BF),
            pltpu.VMEM((256, total), BF),
            pltpu.VMEM((512, 256), BF),
        ),
        cost=cost(4),
        outs=(VMEM, SMEM),
    )
    partner = call(
        permute_kernel, shape(tile, BF), [VMEM] * 2, (slot_pair, held), cost=cost(2), after=(info,)
    )
    arrived = swap(partner)
    coded = call(
        time_mean_kernel,
        shape((blocks, 128, cap), BF),
        [VMEM] * 3,
        (info, time_freq.reshape(1, 128), time_phase.reshape(1, 128)),
        scratch=(
            pltpu.VMEM((blocks * 128, 4 * cap), BF),
            pltpu.VMEM((256, 4 * cap), BF),
            pltpu.VMEM((blocks * 128, 256), F32),
        ),
        cost=cost(1),
    )
    mean = call(
        mean_kernel,
        shape(tile, BF),
        [VMEM] * 2,
        (info, arrived),
        scratch=(pltpu.VMEM((256, total), BF), pltpu.VMEM((256, total), BF)),
        cost=cost(1),
        after=(coded,),
    )
    own_others = call(
        stack_kernel,
        shape((3, blocks + 6, feats, cap), BF),
        [VMEM] * 3,
        own_around,
        cost=cost(1),
        after=(mean,),
    )
    rest = call(
        sorted_gather_kernel,
        shape(tile, BF),
        [VMEM, SMEM, VMEM],
        (info, ranges, low),
        cost=cost(0.05),
    )
    own_full = (own_wide, own_others, other_core(own_wide), other_core(own_others))
    wide, bias = call(
        weights_kernel,
        (shape((4, 48, 128), BF), shape((2, 48, 128), F32)),
        [VMEM] * 6,
        (*own_full, bias_input.reshape(1, 48), bias_hidden.reshape(1, 48)),
        scratch=(pltpu.VMEM((8, 4 * feats, 384), BF),),
        cost=cost(1),
    )
    around = along_z(mean)
    swapped = other_core(mean)
    pre, self_rows = call(
        self_kernel,
        (shape((blocks, 96, cap), F32), shape(tile, BF)),
        [VMEM] * 8,
        (*own_full, info, wide, bias, coded),
        scratch=(
            pltpu.VMEM((blocks * 128, 4 * cap), BF),
            pltpu.VMEM((256, 4 * cap), BF),
            pltpu.VMEM((blocks * 128, 256), F32),
        ),
        cost=cost(0.05),
    )
    others = call(
        stack_kernel, shape((3, *tile), BF), [VMEM] * 3, around, cost=cost(1), after=(pre,)
    )
    swapped_others = other_core(others)
    return call(
        final_kernel,
        shape((feats, nodes), F32),
        [VMEM] * 9 + [SMEM, HBM],
        (
            mean,
            others,
            swapped,
            swapped_others,
            wide,
            pre,
            self_rows,
            rest,
            info,
            ranges,
            memory,
        ),
        scratch=(
            pltpu.VMEM((feats, nodes), F32),
            pltpu.VMEM((blocks, 2 * feats, cap), BF),
            pltpu.VMEM((groups_of * feats, SPAN), F32),
            sems(()),
        ),
        cost=cost(10),
    )


def solution(mesh):
    placed = (
        P("cols", "rows"),
        P("rows"),
        P("rows", None),
        P("rows", None),
        P("rows", None),
        P("rows", None),
        P(),
        P(),
        P("cols", None, None),
        P("cols", None),
        P("cols", None),
        P("cols"),
        P("cols"),
    )
    return jax.shard_map(
        local, mesh=mesh, in_specs=placed, out_specs=P("cols", "rows"), check_vma=False
    )
```

```python
import jax
import jax.numpy as jnp
from jax import lax
from jax.experimental import pallas as pl
from jax.experimental.pallas import tpu as pltpu
from jax.sharding import PartitionSpec as P

BF = jnp.bfloat16
F32 = jnp.float32
I32 = jnp.int32
CAP = 256
SPAN = 1024
WINDOW = 12
VMEM_BYTES = 24 << 20
SCALE = 1.0
SMEM = pl.BlockSpec(memory_space=pltpu.SMEM)
VMEM = pl.BlockSpec(memory_space=pltpu.VMEM)
ANY = pl.BlockSpec(memory_space=pl.ANY)
HBM = pl.BlockSpec(memory_space=pltpu.MemorySpace.HBM)


def call(
    kernel, out_shape, specs, args, scratch=(), cost=None, after=(), vmem=VMEM_BYTES, outs=None
):
    def body(*refs):
        kernel(*refs[len(after) :])

    outs = outs or jax.tree.map(lambda _: VMEM, out_shape)
    return pl.pallas_call(
        body,
        out_shape=out_shape,
        in_specs=[ANY] * len(after) + list(specs),
        out_specs=outs,
        scratch_shapes=list(scratch),
        compiler_params=pltpu.CompilerParams(vmem_limit_bytes=vmem),
        cost_estimate=cost,
    )(*after, *args)


def cost(us):
    return pl.CostEstimate(flops=int(us * SCALE * 1e8), bytes_accessed=int(us * SCALE * 3.5e6), transcendentals=0)


def match(index, rows):
    places = lax.broadcasted_iota(I32, (rows, index.shape[1]), 0).astype(BF)
    return jnp.where(places == index.astype(BF), jnp.ones((), BF), jnp.zeros((), BF))


def match_wide(index, rows):
    parts = [
        match(jnp.where((index >> 8) == k, index & 255, -1), 256) for k in range(rows // 256)
    ]
    return jnp.concatenate(parts, axis=0)


def groups(index, values, count):
    low = index.astype(BF)
    rows = values.shape[0]
    zero = jnp.zeros((), BF)
    return jnp.concatenate(
        [jnp.where(low == jnp.full((rows, 1), k, BF), values, zero) for k in range(count)], axis=0
    )


def dot(a, b):
    return jnp.dot(a, b, preferred_element_type=F32)


def dot_nt(a, b):
    return lax.dot_general(a, b, (((1,), (1,)), ((), ())), preferred_element_type=F32)


def fetch(sems, *pairs):
    copies = [pltpu.make_async_copy(a, b, sems.at[k]) for k, (a, b) in enumerate(pairs)]
    for c in copies:
        c.start()
    for c in copies:
        c.wait()


def rank_of(info, h):
    return info[h, 0:1, :].astype(I32)


def inv_of(info, a):
    return info[a, 1:2, :]


def gap_of(info, h):
    return info[h, 2:3, :]


def node_of(info, a):
    return info[a, 3:4, :].astype(I32)


def send_kernel(count_hbm, node_hbm, tick_hbm, out_ref, count_ref, node_ref, tick_ref, sems, *, nodes):
    fetch(sems, (count_hbm, count_ref), (node_hbm, node_ref), (tick_hbm, tick_ref))
    for b in range(node_ref.shape[0]):
        place = lax.broadcasted_iota(I32, (1, CAP), 1)
        ids = jnp.where(place < count_ref[0, b], node_ref[b : b + 1, :] - b * nodes, nodes)
        out_ref[b, 0:1, :] = ids
        out_ref[b, 1:2, :] = tick_ref[b : b + 1, :]


def prep_kernel(mem_ref, high_ref, low_ref):
    feats = mem_ref.shape[0]
    for g in range(mem_ref.shape[1] // SPAN):
        x = mem_ref[:, g * SPAN : (g + 1) * SPAN]
        high = x.astype(BF)
        high_ref[g * feats : (g + 1) * feats, :] = high
        low_ref[g * feats : (g + 1) * feats, :] = (x - high.astype(F32)).astype(BF)


def gather_kernel(ids_ref, table_ref, out_ref):
    feats = out_ref.shape[1]
    count = table_ref.shape[0] // feats

    def body(h, carry):
        ids = ids_ref[h, 0:1, :]
        high = ids >> 10
        picked = dot(table_ref[...], match_wide(ids & (SPAN - 1), SPAN))
        total = jnp.zeros((feats, CAP), F32)
        for g in range(count):
            total = total + jnp.where(high == g, picked[g * feats : (g + 1) * feats, :], 0.0)
        out_ref[h] = total.astype(BF)
        return carry

    lax.fori_loop(0, ids_ref.shape[0], body, 0, unroll=16)


def own_kernel(ids_ref, table_ref, wp_ref, wt_ref, wh_ref, out_ref, wide_ref):
    gather_kernel(ids_ref, table_ref, out_ref)
    at = out_ref.shape[0]
    wide_ref[0:at] = out_ref[...]
    for m, w in enumerate((wp_ref[:, 0, :], wp_ref[:, 1, :], wt_ref[...], wh_ref[...])):
        wide_ref[at + m] = w[:, 0:256]
        wide_ref[at + 4 + m // 2, :, (m % 2) * 128 : (m % 2 + 1) * 128] = w[:, 256:384]


def sorted_gather_kernel(info_ref, range_ref, table_ref, out_ref):
    feats = out_ref.shape[1]
    count = table_ref.shape[0] // feats

    def window(a, k):
        lowest = range_ref[0, a] + k * WINDOW
        start = jnp.minimum(lowest, count - WINDOW)
        node = node_of(info_ref, a)
        group = node >> 10
        place = jnp.where(group >= lowest, group - start, -1)
        rows = table_ref[pl.ds(pl.multiple_of(start * feats, feats), WINDOW * feats), :]
        picked = dot(rows, match_wide(node & (SPAN - 1), SPAN))
        total = jnp.zeros((feats, CAP), F32)
        for g in range(WINDOW):
            total = total + jnp.where(place == g, picked[g * feats : (g + 1) * feats, :], 0.0)
        return total.astype(BF)

    def first(a, carry):
        out_ref[a] = window(a, 0)
        return carry

    lax.fori_loop(0, out_ref.shape[0], first, 0, unroll=16)

    def others(a, carry):
        def one(k, c):
            out_ref[a] += window(a, k)
            return c

        lax.fori_loop(1, range_ref[1, a], one, 0)
        return carry

    lax.fori_loop(0, out_ref.shape[0], others, 0)


def rank_kernel(ids_ref, last_ref, info_ref, range_ref,
                hi_s, lo_s, left_s, right_s, table_s):
    blocks = ids_ref.shape[0]
    for h in range(blocks):
        ids = ids_ref[h, 0:1, :]
        at = slice(h * CAP, (h + 1) * CAP)
        hi_s[:, at] = match(ids >> 8, 128)
        lo_s[:, at] = match(ids & 255, 256)
    held = dot_nt(hi_s[...], lo_s[...])
    coarse = jnp.floor(held * (1.0 / 64.0))
    fine = (held - 64.0 * coarse).astype(BF)
    coarse = coarse.astype(BF)
    row, col = (lax.broadcasted_iota(I32, (256, 256), d) for d in (0, 1))
    before = jnp.where(row < col, 1.0, 0.0).astype(BF)
    inside = 64.0 * dot(coarse, before) + dot(fine, before)
    row, col = (lax.broadcasted_iota(I32, (128, 128), d) for d in (0, 1))
    above = jnp.where(col < row, 1.0, 0.0).astype(BF)
    ahead = 64.0 * dot(above, coarse) + dot(above, fine)
    ranks = inside + jnp.sum(ahead, axis=1, keepdims=True)
    coarse = jnp.floor(ranks * (1.0 / 64.0))
    fine = (ranks - 64.0 * coarse).astype(BF)
    table_s[0:128] = coarse.astype(BF)
    table_s[128:256] = fine
    for k in range(2):
        last = last_ref[pl.ds(k, 128, stride=2), :]
        at = slice(k * 128, (k + 1) * 128)
        table_s[256:384, at] = (last >> 3).astype(F32).astype(BF)
        table_s[384:512, at] = (last & 7).astype(F32).astype(BF)
    for h in range(blocks):
        ids = ids_ref[h, 0:1, :]
        at = slice(h * CAP, (h + 1) * CAP)
        picked = dot(table_s[...], lo_s[:, at])
        mask = hi_s[:, at].astype(F32)
        both = (64.0 * picked[0:128] + picked[128:256]) * mask
        rank = jnp.sum(both, axis=0, keepdims=True).astype(I32)
        both = (8.0 * picked[256:384] + picked[384:512]) * mask
        info_ref[h, 2:3, :] = ids_ref[h, 1:2, :].astype(F32) - jnp.sum(both, axis=0, keepdims=True)
        rank = jnp.where(ids < 32768, rank, blocks * CAP)
        info_ref[h, 0:1, :] = rank.astype(F32)
        values = jnp.concatenate(
            [
                jnp.ones((1, CAP), F32),
                (ids >> 8).astype(F32),
                (ids & 255).astype(F32),
                jnp.zeros((13, CAP), F32),
            ],
            axis=0,
        ).astype(BF)
        left_s[:, at] = groups(rank >> 8, values, blocks)
        right_s[:, at] = match(rank & 255, 256)
    sums = dot_nt(left_s[...], right_s[...])
    for a in range(blocks):
        n = sums[a * 16 : a * 16 + 1]
        inv = 1.0 / jnp.maximum(n, 1.0)
        high = sums[a * 16 + 1 : a * 16 + 2] * inv + 0.5
        low = sums[a * 16 + 2 : a * 16 + 3] * inv + 0.5
        node = (high.astype(I32) << 8) + low.astype(I32)
        info_ref[a, 1:2, :] = inv
        info_ref[a, 3:4, :] = jnp.where(n > 0.0, node, 32768).astype(F32)
        first = jnp.minimum(jnp.min(jnp.where(n > 0.0, node, 32768)) >> 10, 32 - WINDOW)
        last = jnp.max(jnp.where(n > 0.0, node, 0)) >> 10
        range_ref[0, a] = first
        range_ref[1, a] = 1 + jnp.maximum(last - first, 0) // WINDOW


def permute_kernel(pair_ref, rows_ref, out_ref):
    blocks, feats, _ = rows_ref.shape
    table = rows_ref[...].reshape(blocks * feats, CAP)
    for b in range(blocks):
        pair = pair_ref[b : b + 1, :]
        high = pair >> 8
        picked = dot(table, match(pair & 255, 256))
        total = jnp.zeros((feats, CAP), F32)
        for g in range(blocks):
            total = total + jnp.where(high == g, picked[g * feats : (g + 1) * feats, :], 0.0)
        out_ref[b] = total.astype(BF)


def mean_kernel(info_ref, rows_ref, out_ref, left_s, right_s):
    blocks, feats, _ = rows_ref.shape
    for h in range(blocks):
        rank = rank_of(info_ref, h)
        at = slice(h * CAP, (h + 1) * CAP)
        left_s[:, at] = groups(rank >> 8, rows_ref[h], blocks)
        right_s[:, at] = match(rank & 255, 256)
    sums = dot_nt(left_s[...], right_s[...])
    for a in range(blocks):
        out_ref[a] = (sums[a * feats : (a + 1) * feats] * inv_of(info_ref, a)).astype(BF)


def time_mean_kernel(info_ref, freq_ref, phase_ref, out_ref,
                     left_s, right_s, acc_s):
    blocks, feats, _ = out_ref.shape
    freq = jnp.transpose(jnp.broadcast_to(freq_ref[...], (128, 128)))[:, 0:1]
    phase = jnp.transpose(jnp.broadcast_to(phase_ref[...], (128, 128)))[:, 0:1]
    for q in range(4):
        for i in range(4):
            h = q * 4 + i
            encoded = cosine(gap_of(info_ref, h) * freq + phase).astype(BF)
            at = slice(i * CAP, (i + 1) * CAP)
            left_s[:, at] = groups(rank_of(info_ref, h) >> 8, encoded, blocks)
            right_s[:, at] = match(rank_of(info_ref, h) & 255, 256)
        sums = dot_nt(left_s[...], right_s[...])
        if q == 0:
            acc_s[...] = sums
        elif q < 3:
            acc_s[...] += sums
        else:
            for a in range(blocks):
                at = slice(feats * a, feats * (a + 1))
                out_ref[a] = ((acc_s[at] + sums[at]) * inv_of(info_ref, a)).astype(BF)


def eight(refs):
    return [r for k in (0, 2) for r in (refs[k], *[refs[k + 1].at[i] for i in range(3)])]


def weights_kernel(*refs):
    pieces, (bi_ref, bh_ref, out_ref, bias_ref, all_s) = eight(refs), refs[4:]
    column = lax.axis_index("cols")
    z, side = column >> 1, column & 1
    order = [((z - (k >> 1)) & 3) + 4 * ((k & 1) ^ side) for k in range(8)]
    feats = 16
    for k, piece in enumerate(pieces):
        for m in range(4):
            at = (slice(m * feats, (m + 1) * feats), slice(0, 256))
            all_s[(k, *at)] = piece[16 + m]
            at = (slice(m * feats, (m + 1) * feats), slice(256, 384))
            all_s[(k, *at)] = piece[20 + m // 2, :, (m % 2) * 128 : (m % 2 + 1) * 128]
    out_row = lax.broadcasted_iota(I32, (48, 384), 0)
    source = lax.broadcasted_iota(I32, (48, 384), 1)
    wanted = 48 * column + 3 * (out_row & 15) + (out_row >> 4)
    pick = jnp.where(source == wanted, 1.0, 0.0).astype(BF)
    for m in range(4):
        rows = [
            all_s[order[k] if m == 2 else k, m * feats : (m + 1) * feats, :] for k in range(8)
        ]
        out_ref[m] = dot_nt(pick, jnp.concatenate(rows, axis=0)).astype(BF)
    out_row = lax.broadcasted_iota(I32, (48, 48), 0)
    source = lax.broadcasted_iota(I32, (48, 48), 1)
    same = source == 3 * (out_row & 15) + (out_row >> 4)
    for k, ref in enumerate((bi_ref, bh_ref)):
        column_of = jnp.sum(jnp.where(same, ref[...], 0.0), axis=1, keepdims=True)
        bias_ref[k] = jnp.broadcast_to(column_of, (48, 128))


def cosine(x):
    turns = jnp.floor(x * 0.15915494309189535 + 0.5)
    u = 0.5 * x - turns * 3.140625
    u = u - turns * 9.67653589793e-4
    s = u * u
    q = s * -2.50521084e-08 + 2.75573192e-06
    q = q * s - 1.98412698e-04
    q = q * s + 8.33333333e-03
    q = q * s - 1.66666667e-01
    sine = u + u * s * q
    return 1.0 - 2.0 * sine * sine


def stack_kernel(p1, p2, p3, out_ref):
    for k, p in enumerate((p1, p2, p3)):
        out_ref[k] = p[...]


def self_kernel(*refs):
    pieces = eight(refs)
    info_ref, w_ref, bias_ref, code_ref, out_ref, own_ref = refs[4:10]
    left_s, right_s, acc_s = refs[10:]
    blocks, feats, _ = own_ref.shape
    rows = 8 * feats
    for q in range(4):
        for i in range(4):
            h = q * 4 + i
            full = jnp.concatenate([p[h] for p in pieces], axis=0)
            at = slice(i * CAP, (i + 1) * CAP)
            left_s[:, at] = groups(rank_of(info_ref, h) >> 8, full, blocks)
            right_s[:, at] = match(rank_of(info_ref, h) & 255, 256)
        sums = dot_nt(left_s[...], right_s[...])
        if q == 0:
            acc_s[...] = sums
        elif q < 3:
            acc_s[...] += sums
        else:
            for a in range(blocks):
                at = slice(rows * a, rows * (a + 1))
                full = ((acc_s[at] + sums[at]) * inv_of(info_ref, a)).astype(BF)
                own_ref[a] = full[0:feats]
                gx = dot(w_ref[0], full) + dot(w_ref[2], code_ref[a])
                out_ref[a, 0:48] = gx + bias_ref[0, :, 0:1]
                out_ref[a, 48:96] = dot(w_ref[3], full) + bias_ref[1, :, 0:1]


def final_kernel(*refs):
    pieces = eight(refs)
    w_ref, pre_ref, high_ref, low_ref, info_ref, range_ref, mem_hbm, out_ref = refs[4:12]
    mem_ref, change_s, acc_s, sem = refs[12:]
    load = pltpu.make_async_copy(mem_hbm, mem_ref, sem)
    load.start()
    blocks, feats, _ = low_ref.shape
    count = mem_ref.shape[1] // SPAN
    span = WINDOW * feats
    acc_s[...] = jnp.zeros_like(acc_s)

    def gates(a, carry):
        full = jnp.concatenate([p[a] for p in pieces], axis=0)
        gx = pre_ref[a, 0:48] + dot(w_ref[1], full)
        gh = pre_ref[a, 48:96]
        reset = jax.nn.sigmoid(gx[0:16] + gh[0:16])
        keep = jax.nn.sigmoid(gx[16:32] + gh[16:32])
        cand = jnp.tanh(gx[32:48] + reset * gh[32:48])
        hidden = high_ref[a].astype(F32) + low_ref[a].astype(F32)
        change = (1.0 - keep) * (cand - hidden)
        high = change.astype(BF)
        change_s[a, 0:feats] = high
        change_s[a, feats : 2 * feats] = (change - high.astype(F32)).astype(BF)
        return carry

    lax.fori_loop(0, blocks, gates, 0, unroll=16)

    def add_window(a, k):
        lowest = range_ref[0, a] + k * WINDOW
        start = jnp.minimum(lowest, count - WINDOW)
        node = node_of(info_ref, a)
        group = node >> 10
        place = jnp.where(group >= lowest, group - start, -1)
        spread = match_wide(node & (SPAN - 1), SPAN)
        left = [
            groups(place, change_s[a, f * feats : (f + 1) * feats], WINDOW) for f in range(2)
        ]
        sums = dot_nt(jnp.concatenate(left, axis=0), spread)
        at = pl.ds(pl.multiple_of(start * feats, feats), span)
        acc_s[at, :] += sums[:span] + sums[span:]

    def first_windows(a, carry):
        add_window(a, 0)
        return carry

    lax.fori_loop(0, blocks, first_windows, 0, unroll=16)

    def other_windows(a, carry):
        def one(k, c):
            add_window(a, k)
            return c

        lax.fori_loop(1, range_ref[1, a], one, 0)
        return carry

    lax.fori_loop(0, blocks, other_windows, 0)
    load.wait()
    for g in range(count):
        at = slice(g * SPAN, (g + 1) * SPAN)
        out_ref[:, at] = mem_ref[:, at] + acc_s[g * feats : (g + 1) * feats, :]


def shape(s, d):
    return jax.ShapeDtypeStruct(s, d)


def local(
    memory,
    last_tick,
    slot_node,
    slot_pair,
    slot_tick,
    block_count,
    time_freq,
    time_phase,
    w_pair,
    w_time,
    w_hidden,
    bias_input,
    bias_hidden,
):
    feats, nodes = memory.shape
    blocks, cap = slot_node.shape
    total = blocks * cap
    tile = (blocks, feats, cap)

    def along_z(x):
        return [
            lax.ppermute(x, "cols", [(j, ((j // 2 + d) % 4) * 2 + j % 2) for j in range(8)])
            for d in (1, 2, 3)
        ]

    def other_core(x):
        return lax.ppermute(x, "cols", [(j, j ^ 1) for j in range(8)])

    def swap(x):
        return lax.all_to_all(x, "rows", split_axis=0, concat_axis=0, tiled=True)

    sems = pltpu.SemaphoreType.DMA
    asked = call(
        lambda *r: send_kernel(*r, nodes=nodes),
        shape((blocks, 2, cap), I32),
        [HBM] * 3,
        (block_count, slot_node, slot_tick),
        scratch=(
            pltpu.SMEM((1, blocks), I32),
            pltpu.VMEM((blocks, cap), I32),
            pltpu.VMEM((blocks, cap), I32),
            sems((3,)),
        ),
        cost=cost(2),
        vmem=60 << 20,
    )
    groups_of = nodes // SPAN
    table = shape((groups_of * feats, SPAN), BF)
    high, low = call(
        prep_kernel, (table, table), [VMEM], (memory,), cost=cost(1), after=(asked,)
    )
    asked = swap(asked)
    own, own_wide = call(
        own_kernel,
        (shape(tile, BF), shape((blocks + 6, feats, cap), BF)),
        [VMEM] * 5,
        (asked, high, w_pair, w_time, w_hidden),
        cost=cost(7),
    )
    own_around = along_z(own_wide)
    held = swap(own)
    info, ranges = call(
        rank_kernel,
        (
            shape((blocks, 4, cap), F32),
            shape((2, blocks), I32),
        ),
        [VMEM] * 2,
        (asked, last_tick.reshape(nodes // 128, 128)),
        scratch=(
            pltpu.VMEM((128, total), BF),
            pltpu.VMEM((256, total), BF),
            pltpu.VMEM((256, total), BF),
            pltpu.VMEM((256, total), BF),
            pltpu.VMEM((512, 256), BF),
        ),
        cost=cost(4),
        outs=(VMEM, SMEM),
    )
    partner = call(
        permute_kernel, shape(tile, BF), [VMEM] * 2, (slot_pair, held), cost=cost(2), after=(info,)
    )
    arrived = swap(partner)
    coded = call(
        time_mean_kernel,
        shape((blocks, 128, cap), BF),
        [VMEM] * 3,
        (info, time_freq.reshape(1, 128), time_phase.reshape(1, 128)),
        scratch=(
            pltpu.VMEM((blocks * 128, 4 * cap), BF),
            pltpu.VMEM((256, 4 * cap), BF),
            pltpu.VMEM((blocks * 128, 256), F32),
        ),
        cost=cost(1),
    )
    mean = call(
        mean_kernel,
        shape(tile, BF),
        [VMEM] * 2,
        (info, arrived),
        scratch=(pltpu.VMEM((256, total), BF), pltpu.VMEM((256, total), BF)),
        cost=cost(1),
        after=(coded,),
    )
    own_others = call(
        stack_kernel,
        shape((3, blocks + 6, feats, cap), BF),
        [VMEM] * 3,
        own_around,
        cost=cost(1),
        after=(mean,),
    )
    rest = call(
        sorted_gather_kernel,
        shape(tile, BF),
        [VMEM, SMEM, VMEM],
        (info, ranges, low),
        cost=cost(0.05),
    )
    own_full = (own_wide, own_others, other_core(own_wide), other_core(own_others))
    wide, bias = call(
        weights_kernel,
        (shape((4, 48, 128), BF), shape((2, 48, 128), F32)),
        [VMEM] * 6,
        (*own_full, bias_input.reshape(1, 48), bias_hidden.reshape(1, 48)),
        scratch=(pltpu.VMEM((8, 4 * feats, 384), BF),),
        cost=cost(1),
    )
    around = along_z(mean)
    swapped = other_core(mean)
    pre, self_rows = call(
        self_kernel,
        (shape((blocks, 96, cap), F32), shape(tile, BF)),
        [VMEM] * 8,
        (*own_full, info, wide, bias, coded),
        scratch=(
            pltpu.VMEM((blocks * 128, 4 * cap), BF),
            pltpu.VMEM((256, 4 * cap), BF),
            pltpu.VMEM((blocks * 128, 256), F32),
        ),
        cost=cost(0.05),
    )
    others = call(
        stack_kernel, shape((3, *tile), BF), [VMEM] * 3, around, cost=cost(1), after=(pre,)
    )
    swapped_others = other_core(others)
    return call(
        final_kernel,
        shape((feats, nodes), F32),
        [VMEM] * 9 + [SMEM, HBM],
        (
            mean,
            others,
            swapped,
            swapped_others,
            wide,
            pre,
            self_rows,
            rest,
            info,
            ranges,
            memory,
        ),
        scratch=(
            pltpu.VMEM((feats, nodes), F32),
            pltpu.VMEM((blocks, 2 * feats, cap), BF),
            pltpu.VMEM((groups_of * feats, SPAN), F32),
            sems(()),
        ),
        cost=cost(10),
    )


def solution(mesh):
    placed = (
        P("cols", "rows"),
        P("rows"),
        P("rows", None),
        P("rows", None),
        P("rows", None),
        P("rows", None),
        P(),
        P(),
        P("cols", None, None),
        P("cols", None),
        P("cols", None),
        P("cols"),
        P("cols"),
    )
    return jax.shard_map(
        local, mesh=mesh, in_specs=placed, out_specs=P("cols", "rows"), check_vma=False
    )
```
